32 devices in a mesh: case: 2 (over x), mesh: 8 (over z, y), harm: 2 (over core).
Axes of the slice: x: 2, y: 2, z: 4, core: 2. Of those that a mesh axis runs over, the one named last changes fastest.
Arguments:
- coeffs: float32 [64, 3, 16384], P('harm', None, ('case', 'mesh')), parts along dimension 2, may hold values from -0.2 to 0.2
- load: float32 [64, 3, 16384], P('harm', None, ('case', 'mesh')), parts along dimension 2, may hold values from -2 to 2
- mass: float32 [8192], P('mesh'), may hold values from 0.3 to 3
- stiffness: float32 [16384], P('mesh'), may hold values from 0.3 to 3
- edge_ref: float32 [2, 3, 16384], P(None, None, 'mesh'), may hold values from -4 to 4
- conn: int32 [3, 16384], P(None, 'mesh'), may hold values from 0 to 1151, as said below
- ghost_send: int32 [2, 512], P(None, 'mesh'), may hold values from 0 to 1023
- order: int32 [64], replicated, may hold values from 0 to 63, each once
- basis: bfloat16 [256, 3, 8192], P(None, None, 'mesh'), may hold values from -0.0546875 to 0.0546875
Outputs:
- resid: float32 [64, 3, 16384], P('harm', None, ('case', 'mesh')), parts along dimension 2
- reduced: float32 [256, 128], P('mesh', ('case', 'harm')), parts along dimension 1
The draws below stay inside these ranges and needn't reach their ends.
There are 2 independent parts, one for each index of `case`. The reference program is written for one: setup_inputs(seed, part) draws one part's arguments, and reference() takes and returns one part's arrays. A program takes and returns all parts, laid end to end along the dimension named above; an argument that names none is the same for every part. Nothing has to cross between parts.
Inputs may be any that keep to these rules, and one draw needn't show every extreme that they name: `conn`: A triangle of the first block refers to no lower neighbour node slot, one of the last block to no upper one; slots 1024 to 1087 name the lower neighbour's shared nodes, the rest the upper neighbour's.
All inputs are finite; a program needn't handle non-finite values.
Results may differ from the reference program's by a relative error of at most 0.003.
Values sent between devices are 32-bit elements; how exact they have to be, the bound alone decides.
A program may use at most 64 MiB of HBM per device.

```python
import math
import jax
import jax.numpy as jnp
from jax import lax

COEF = 64
BASIS = 256
NODE_DEV = 1024
GHOST = 64
ELEM_DEV = 2048
NODES = 8192
ELEMS = 16384
N_MESH = 8


def draw_conn(key, part):
    key = jax.random.fold_in(key, 11)
    key_first, key_other = jax.random.split(key, 2)
    first_ref = jax.random.randint(key_first, (1, ELEMS), 0, NODE_DEV)
    other_ref = jax.random.randint(key_other, (2, ELEMS), 0, NODE_DEV + 2 * GHOST)
    block = jnp.arange(ELEMS) // ELEM_DEV
    last_block = ELEMS // ELEM_DEV - 1
    lower_slot = (other_ref >= NODE_DEV) & (other_ref < NODE_DEV + GHOST)
    upper_slot = other_ref >= NODE_DEV + GHOST
    other_ref = jnp.where((block[None, :] == 0) & lower_slot, other_ref - NODE_DEV, other_ref)
    other_ref = jnp.where((block[None, :] == last_block) & upper_slot, other_ref - NODE_DEV - GHOST, other_ref)
    other_ref = other_ref.at[1, ELEM_DEV].set(NODE_DEV + 2 * GHOST - 1)
    first_ref = first_ref.at[0, 0].set(0)
    return jnp.concatenate([first_ref, other_ref], 0).astype(jnp.int32)


def plant(drawn, key, least, high):
    dims = drawn.shape
    place = [jax.random.randint(jax.random.fold_in(key, axis), (), 0, dims[axis]) for axis in range(len(dims))]
    drawn = drawn.at[tuple(place)].set(least)
    longest = dims.index(max(dims))
    place[longest] = (place[longest] + 1) % dims[longest]
    return drawn.at[tuple(place)].set(high)


def strengthened(values, own_key, source, target, blocks, factor):
    owner, partner = [(jnp.arange(values.shape[axis_at]) // (values.shape[axis_at] // blocks)).reshape([-1 if axis == axis_at else 1 for axis in range(values.ndim)]) for axis_at in (source, target)]
    chosen = jax.random.permutation(own_key, blocks)[partner]
    strong = (owner == chosen) | (owner == (partner + blocks // 2) % blocks)
    return jnp.where(strong, factor * values, values)


def level_of(own_key, dims, pieces, low, top_value):
    def one(dim, parts):
        heights = jax.random.uniform(jax.random.fold_in(jax.random.fold_in(own_key, 6), dim), (parts,), jnp.float32, low / len(pieces), top_value / len(pieces))
        return jnp.repeat(jnp.exp(heights), dims[dim] // parts).reshape((-1,) + (1,) * (len(dims) - dim - 1))

    level = one(*pieces[0])
    for cut in pieces[1:]:
        level = level * one(*cut)
    return level


def normal_values(rng, dims, spread, reach, shards=(), held_as=jnp.bfloat16):
    drawn = jax.random.normal(rng, dims, jnp.float32) * spread
    if len(shards) > 0:
        drawn = level_of(rng, dims, shards, -0.22, 0.18) * drawn
    return jnp.clip(drawn, min=-reach, max=reach).astype(held_as)


def heavy_noise(rng, extent, spread, most, pieces, heavy, held_as=jnp.bfloat16):
    result = spread * jax.random.normal(rng, extent, jnp.float32)
    if pieces:
        result = result * level_of(rng, extent, pieces, -0.22, 0.18)
    return jnp.clip(strengthened(result, jax.random.fold_in(rng, 3), *heavy), -most, most).astype(held_as)


def setup_inputs(seed: int = 0, part: int = 0) -> dict:
    key_of = jax.random.split(jax.random.key(seed), 10)
    part_splits = jax.random.split(jax.random.fold_in(key_of[9], part), 10)
    coeffs = normal_values(part_splits[0], (COEF, 3, NODES), 0.03, 0.2, ((0, 2), (2, 8)), jnp.float32)
    load = normal_values(part_splits[1], (COEF, 3, NODES), 0.3, 2.0, ((0, 2), (2, 8)), jnp.float32)
    mass = jnp.clip(jnp.exp(math.log(3.0) - 2.3025851 * jax.random.uniform(key_of[2], (NODES,), jnp.float32) ** level_of(key_of[2], (NODES,), ((0, 8),), -0.2, 0.2)), 0.3, 3.0)
    stiffness = jnp.clip(jnp.exp(math.log(3.0) - 2.3025851 * jax.random.uniform(key_of[3], (ELEMS,), jnp.float32) ** level_of(key_of[3], (ELEMS,), ((0, 8),), -0.2, 0.2)), 0.3, 3.0)
    edge_ref = normal_values(key_of[4], (2, 3, ELEMS), 0.7, 4.0, ((2, 8),), jnp.float32)
    conn = draw_conn(jax.random.fold_in(key_of[9], 71), part)
    ghost_send = plant(jax.random.randint(key_of[6], (2, N_MESH * GHOST), 0, NODE_DEV), jax.random.fold_in(key_of[6], 1), 0, NODE_DEV - 1).astype(jnp.int32)
    order = jax.random.permutation(key_of[7], COEF).astype(jnp.int32)
    basis = heavy_noise(key_of[8], (BASIS, 3, NODES), (3 * NODES) ** -0.5, 0.0546875, ((2, 8),), (2, 0, 8, 2.0))
    return {"coeffs": coeffs, "load": load, "mass": mass, "stiffness": stiffness, "edge_ref": edge_ref, "conn": conn, "ghost_send": ghost_send, "order": order, "basis": basis}


OMEGA = 0.1
PRESTRESS = 0.2


def fourier_tables(order, ncoef):
    samples = jnp.arange(ncoef, dtype=jnp.int32)
    which = order.astype(jnp.int32)
    harmonic = (which + 1) // 2
    phase = (harmonic[:, None] * samples[None, :]) % ncoef
    angle = (2.0 * math.pi / ncoef) * phase.astype(jnp.float32)
    cosine = (which % 2 == 1) | (which == 0)
    synth = jnp.where(cosine[:, None], jnp.cos(angle), jnp.sin(angle))
    weight = jnp.where((which == 0) | (which == ncoef - 1), 1.0, 2.0) / ncoef
    proj = synth * weight[:, None]
    freq = (OMEGA * harmonic.astype(jnp.float32)) ** 2
    return synth, proj, freq


def edge_force(stiffness, ref_edge, start_disp, end_disp):
    stretch = ref_edge + end_disp - start_disp
    tension = stiffness * (0.5 * (jnp.sum(stretch * stretch, 0) - jnp.sum(ref_edge * ref_edge, 0)) + PRESTRESS)
    return tension[None, :] * stretch


def reference(coeffs, load, mass, stiffness, edge_ref, conn, ghost_send, order, basis):
    synth, proj, freq = fourier_tables(order, COEF)
    disp = jnp.dot(synth.T, coeffs.reshape(COEF, -1), precision=lax.Precision.HIGHEST).reshape(COEF, 3, NODES)
    block = jnp.arange(ELEMS, dtype=jnp.int32) // ELEM_DEV
    limit = N_MESH * GHOST - 1

    def globalize(local_ref):
        own_node = block * NODE_DEV + local_ref
        lower_slot = jnp.clip((block - 1) * GHOST + local_ref - NODE_DEV, 0, limit).astype(jnp.int32)
        lower_node = (block - 1) * NODE_DEV + ghost_send[1][lower_slot]
        upper_slot = jnp.clip((block + 1) * GHOST + local_ref - NODE_DEV - GHOST, 0, limit).astype(jnp.int32)
        upper_node = (block + 1) * NODE_DEV + ghost_send[0][upper_slot]
        chosen = jnp.where(local_ref < NODE_DEV, own_node, jnp.where(local_ref < NODE_DEV + GHOST, lower_node, upper_node))
        return chosen.astype(jnp.int32)

    node_first = globalize(conn[0])
    node_second = globalize(conn[1])
    node_third = globalize(conn[2])
    edge_one = edge_ref[0]
    edge_two = edge_ref[1]

    def force_sample(sample):
        disp_first = sample[:, node_first]
        disp_second = sample[:, node_second]
        disp_third = sample[:, node_third]
        force_ab = edge_force(stiffness, edge_one, disp_first, disp_second)
        force_ac = edge_force(stiffness, edge_two, disp_first, disp_third)
        force_bc = edge_force(stiffness, edge_two - edge_one, disp_second, disp_third)
        summed = jnp.zeros((3, NODES), jnp.float32)
        summed = summed.at[:, node_first].add(-force_ab - force_ac)
        summed = summed.at[:, node_second].add(force_ab - force_bc)
        summed = summed.at[:, node_third].add(force_ac + force_bc)
        return summed

    internal = lax.map(force_sample, disp)
    force_coef = jnp.dot(proj, internal.reshape(COEF, -1), precision=lax.Precision.HIGHEST).reshape(COEF, 3, NODES)
    resid = force_coef - freq[:, None, None] * mass[None, None, :] * coeffs - load
    resid_low = resid.astype(jnp.bfloat16)
    reduced = lax.dot_general(basis.reshape(BASIS, -1), resid_low.reshape(COEF, -1), (((1,), (1,)), ((), ())), preferred_element_type=jnp.float32)
    return resid, reduced
```

```python
import math

import jax
import jax.numpy as jnp
from jax import lax
from jax.experimental import pallas as pl
from jax.experimental.pallas import tpu as pltpu
from jax.sharding import PartitionSpec as P

OMEGA = 0.1
PRESTRESS = 0.2
F32 = jnp.float32
BF16 = jnp.bfloat16
MESH = pl.DeviceIdType.MESH
LANES = 256


def halves(x):
    high = x.astype(BF16)
    return high, (x - high.astype(F32)).astype(BF16)


def dot(a, b):
    return jnp.dot(a, b, preferred_element_type=F32)


def dot_t(a, b):
    return lax.dot_general(a, b, (((1,), (1,)), ((), ())), preferred_element_type=F32)


def wave(order, samples, ncoef):
    harmonic = (order + 1) // 2
    phase = (harmonic * samples) % ncoef
    angle = (2.0 * math.pi / ncoef) * phase.astype(F32)
    cosine = (order % 2 == 1) | (order == 0)
    return jnp.where(cosine, jnp.cos(angle), jnp.sin(angle))


def kernel(
    n_mesh,
    coef_ref, load_hbm, mass_ref, stiff_ref, edge_ref, conn_ref, ghost_ref, order_ref, basis_hbm,
    resid_ref, reduced_ref,
    load_ref, basis_ref, coef_in, own_hl, other_hl, pick, inc, ghost_out, ghost_in, ghost_hl,
    edge_own, edge_hl, disp, force_hl, coef_hl, back_out, back_in, part_out, part_in, main_own, low,
    prod_out, prod_in,
    local_sem, coef_sem, ghost_send_sem, ghost_recv_sem, part_sem,
    back_send_sem, back_recv_sem, prod_send_sem, prod_recv_sem,
):
    rows, nodes = coef_ref.shape
    block = rows // 3
    ncoef = 2 * block
    ghosts = ghost_ref.shape[1]
    elems = conn_ref.shape[1] // 2
    slots = nodes + 2 * ghosts
    share = prod_out.shape[1]
    me = lax.axis_index("mesh")
    harm = lax.axis_index("harm")
    other = 1 - harm
    has_low, has_up = me > 0, me < n_mesh - 1

    barrier = pltpu.get_barrier_semaphore()
    pl.semaphore_signal(barrier, inc=1, device_id={"harm": other}, device_id_type=MESH)
    for step in range(1, n_mesh):
        pl.semaphore_signal(
            barrier, inc=1, device_id={"mesh": lax.rem(me + step, n_mesh)}, device_id_type=MESH
        )

    @pl.when(has_low)
    def _():
        pl.semaphore_signal(
            barrier, inc=1, device_id={"mesh": me - 1, "harm": other}, device_id_type=MESH
        )

    @pl.when(has_up)
    def _():
        pl.semaphore_signal(
            barrier, inc=1, device_id={"mesh": me + 1, "harm": other}, device_id_type=MESH
        )

    load_copy = pltpu.make_async_copy(load_hbm, load_ref, local_sem.at[0])
    basis_copy = pltpu.make_async_copy(basis_hbm, basis_ref, local_sem.at[1])
    load_copy.start()
    basis_copy.start()

    high, lower = halves(coef_ref[...])
    own_hl[0:rows, :] = high
    own_hl[rows : 2 * rows, :] = lower
    shared = jnp.concatenate([ghost_ref[1:2, :], ghost_ref[0:1, :]], axis=1)
    node_ids = lax.broadcasted_iota(jnp.int32, (nodes, 2 * ghosts), 0)
    pick[...] = jnp.where(node_ids == shared, 1.0, 0.0).astype(BF16)
    picked = dot(own_hl[...], pick[...])
    ghost_out[...] = picked[0:rows] + picked[rows : 2 * rows]

    arrivals = n_mesh + has_low.astype(jnp.int32) + has_up.astype(jnp.int32)
    pl.semaphore_wait(barrier, arrivals)

    coef_copy = pltpu.make_async_remote_copy(
        src_ref=coef_ref, dst_ref=coef_in, send_sem=coef_sem.at[0], recv_sem=coef_sem.at[1],
        device_id={"harm": other}, device_id_type=MESH,
    )
    coef_copy.start()

    def border(src, dst, send_sem, recv_sem, side, rel):
        return pltpu.make_async_remote_copy(
            src_ref=src, dst_ref=dst.at[side, rel], send_sem=send_sem.at[side, rel],
            recv_sem=recv_sem.at[side, rel],
            device_id={
                "mesh": me + 1 if side == 0 else me - 1, "harm": harm if rel == 0 else other,
            },
            device_id_type=MESH,
        )

    there = (has_up, has_low)
    come = (has_low, has_up)

    def border_start(src, dst, send_sem, recv_sem, rel):
        for side in (0, 1):
            @pl.when(there[side])
            def _():
                border(src, dst, send_sem, recv_sem, side, rel).start()

    def border_wait_recv(src, dst, send_sem, recv_sem, rel):
        for side in (0, 1):
            @pl.when(come[side])
            def _():
                border(src, dst, send_sem, recv_sem, side, rel).wait_recv()

            @pl.when(jnp.logical_not(come[side]))
            def _():
                dst[side, rel] = jnp.zeros(dst.shape[2:], F32)

    def border_wait_send(src, dst, send_sem, recv_sem, rel):
        for side in (0, 1):
            @pl.when(there[side])
            def _():
                border(src, dst, send_sem, recv_sem, side, rel).wait_send()

    ghost_args = (ghost_out, ghost_in, ghost_send_sem, ghost_recv_sem)
    border_start(*ghost_args, 0)
    border_start(*ghost_args, 1)

    mine = pl.ds(pl.multiple_of(harm * elems, elems), elems)
    step_rows = 64

    def fill(k, _):
        base = pl.multiple_of(k * step_rows, step_rows)
        for at in range(0, elems, LANES):
            cols = pl.ds(pl.multiple_of(harm * elems + at, LANES), LANES)
            ids = lax.broadcasted_iota(jnp.int32, (step_rows, LANES), 0) + base
            first = jnp.where(ids == conn_ref[0:1, cols], 1.0, 0.0)
            second = jnp.where(ids == conn_ref[1:2, cols], 1.0, 0.0)
            third = jnp.where(ids == conn_ref[2:3, cols], 1.0, 0.0)
            inc[pl.ds(base, step_rows), at : at + LANES] = (second - first).astype(BF16)
            inc[pl.ds(base, step_rows), elems + at : elems + at + LANES] = (third - first).astype(BF16)
        return 0

    lax.fori_loop(0, slots // step_rows, fill, 0)

    row = order_ref[...]
    row = jnp.where(harm == 0, row, jnp.concatenate([row[:, block:], row[:, :block]], axis=1))
    row3 = jnp.concatenate([row, row, row], axis=1)
    synth = wave(row3, lax.broadcasted_iota(jnp.int32, (ncoef, 3 * ncoef), 0), ncoef)
    third_part = lax.broadcasted_iota(jnp.int32, (ncoef, 3 * ncoef), 1) >= 2 * ncoef
    high, lower = halves(synth)
    synth3 = jnp.where(third_part, lower.astype(F32), high.astype(F32)).astype(BF16)
    eye = lax.broadcasted_iota(jnp.int32, (ncoef, ncoef), 0) == lax.broadcasted_iota(
        jnp.int32, (ncoef, ncoef), 1
    )
    column = jnp.sum(jnp.where(eye, row.astype(F32), 0.0), axis=1, keepdims=True).astype(jnp.int32)
    samples = lax.broadcasted_iota(jnp.int32, (ncoef, 3 * ncoef), 1) % ncoef
    weight = jnp.where((column == 0) | (column == ncoef - 1), 1.0, 2.0) / ncoef
    high, lower = halves(wave(column, samples, ncoef) * weight)
    proj3 = jnp.where(third_part, lower.astype(F32), high.astype(F32)).astype(BF16)
    freq = (OMEGA * ((column[0:block] + 1) // 2).astype(F32)) ** 2

    for at in range(0, 2 * elems, LANES):
        edge_own[:, at : at + LANES] = dot(own_hl[...], inc[0:nodes, at : at + LANES])

    coef_copy.wait_recv()
    high, lower = halves(coef_in[...])
    other_hl[0:rows, 0:nodes] = high
    other_hl[rows : 2 * rows, 0:nodes] = lower
    lane = lax.broadcasted_iota(jnp.int32, (rows, 2 * ghosts), 1)
    border_wait_recv(*ghost_args, 0)
    border_wait_recv(*ghost_args, 1)
    high, lower = halves(jnp.where(lane < ghosts, ghost_in[0, 0], ghost_in[1, 0]))
    ghost_hl[0:rows, :] = high
    ghost_hl[rows : 2 * rows, :] = lower
    high, lower = halves(jnp.where(lane < ghosts, ghost_in[0, 1], ghost_in[1, 1]))
    other_hl[0:rows, nodes:slots] = high
    other_hl[rows : 2 * rows, nodes:slots] = lower

    for at in range(0, 2 * elems, LANES):
        cols = slice(at, at + LANES)
        mine_edges = edge_own[:, cols] + dot(ghost_hl[...], inc[nodes:slots, cols])
        other_edges = dot(other_hl[...], inc[:, cols])
        for half, edges in enumerate((mine_edges, other_edges)):
            high, lower = halves(edges[0:rows] + edges[rows : 2 * rows])
            for c in range(3):
                part = slice(c * block, (c + 1) * block)
                for third, piece in enumerate((high, lower, high)):
                    top = third * ncoef + half * block
                    edge_hl[c, top : top + block, cols] = piece[part]
    for c in range(3):
        for at in range(0, 2 * elems, LANES):
            cols = slice(at, at + LANES)
            disp[c, :, cols] = dot(synth3, edge_hl[c, :, cols])

    def sample_rows(k, _):
        base = pl.multiple_of(k * 16, 16)
        times = pl.ds(base, 16)
        for at in range(0, elems, LANES):
            cols = pl.ds(pl.multiple_of(harm * elems + at, LANES), LANES)
            stiff = stiff_ref[0:1, cols]
            refs_b = [edge_ref[c, 0:1, cols] for c in range(3)]
            refs_c = [edge_ref[c, 1:2, cols] for c in range(3)]
            refs_d = [x - y for x, y in zip(refs_c, refs_b)]

            def pull(stretch, refs):
                rest = refs[0] * refs[0] + refs[1] * refs[1] + refs[2] * refs[2]
                square = stretch[0] * stretch[0] + stretch[1] * stretch[1] + stretch[2] * stretch[2]
                return stiff * (0.5 * (square - rest) + PRESTRESS)

            str_b = [refs_b[c] + disp[c, times, at : at + LANES] for c in range(3)]
            str_c = [refs_c[c] + disp[c, times, elems + at : elems + at + LANES] for c in range(3)]
            str_d = [x - y for x, y in zip(str_c, str_b)]
            ten_b = pull(str_b, refs_b)
            ten_c = pull(str_c, refs_c)
            ten_d = pull(str_d, refs_d)
            for c in range(3):
                mid = ten_d * str_d[c]
                for which, value in enumerate((ten_b * str_b[c] - mid, ten_c * str_c[c] + mid)):
                    high, lower = halves(value)
                    to = slice(which * elems + at, which * elems + at + LANES)
                    force_hl[c, times, to] = high
                    force_hl[c, pl.ds(base + ncoef, 16), to] = lower
                    force_hl[c, pl.ds(base + 2 * ncoef, 16), to] = high
        return 0

    lax.fori_loop(0, ncoef // 16, sample_rows, 0)

    for c in range(3):
        for at in range(0, 2 * elems, LANES):
            cols = slice(at, at + LANES)
            value = dot(proj3, force_hl[c, :, cols])
            high, lower = halves(value)
            for half in (0, 1):
                part = slice(half * block, (half + 1) * block)
                coef_hl[half, c * block : (c + 1) * block, cols] = high[part]
                coef_hl[half, rows + c * block : rows + (c + 1) * block, cols] = lower[part]

    def spread(half, start, stop):
        summed = dot_t(coef_hl[half], inc[start:stop, :])
        return summed[0:rows] + summed[rows : 2 * rows]

    back_args = [
        (back_out.at[rel], back_in, back_send_sem, back_recv_sem, rel) for rel in (0, 1)
    ]
    back_out[1] = spread(1, nodes, slots)
    border_start(*back_args[1])
    back_out[0] = spread(0, nodes, slots)
    border_start(*back_args[0])
    for at in range(0, nodes, LANES):
        part_out[:, at : at + LANES] = spread(1, at, at + LANES)
    part_copy = pltpu.make_async_remote_copy(
        src_ref=part_out, dst_ref=part_in, send_sem=part_sem.at[0], recv_sem=part_sem.at[1],
        device_id={"harm": other}, device_id_type=MESH,
    )
    part_copy.start()
    load_copy.wait()
    for at in range(0, nodes, LANES):
        cols = slice(at, at + LANES)
        main_own[:, cols] = spread(0, at, at + LANES)

    border_wait_recv(*back_args[0])
    border_wait_recv(*back_args[1])
    back = jnp.where(lane < ghosts, back_in[1, 0] + back_in[1, 1], back_in[0, 0] + back_in[0, 1])
    high, lower = halves(back)
    ghost_hl[0:rows, :] = high
    ghost_hl[rows : 2 * rows, :] = lower
    part_copy.wait_recv()
    for at in range(0, nodes, LANES):
        cols = slice(at, at + LANES)
        added = dot_t(ghost_hl[...], pick[at : at + LANES, :])
        forces = main_own[:, cols] + part_in[:, cols] + (added[0:rows] + added[rows : 2 * rows])
        for c in range(3):
            part = slice(c * block, (c + 1) * block)
            inertia = freq * mass_ref[0:1, cols] * coef_ref[part, cols]
            value = forces[part] - inertia - load_ref[part, cols]
            resid_ref[part, cols] = value
            low[c, :, cols] = value.astype(BF16)

    basis_copy.wait()
    total = None
    for c in range(3):
        term = dot_t(basis_ref[c], low[c])
        total = term if total is None else total + term
    for piece in range(n_mesh):
        prod_out[piece] = total[piece * share : (piece + 1) * share]

    prod_copies = []
    for step in range(1, n_mesh):
        peer = lax.rem(me + step, n_mesh)
        copy = pltpu.make_async_remote_copy(
            src_ref=prod_out.at[peer], dst_ref=prod_in.at[step - 1],
            send_sem=prod_send_sem.at[step - 1], recv_sem=prod_recv_sem.at[step - 1],
            device_id={"mesh": peer}, device_id_type=MESH,
        )
        copy.start()
        prod_copies.append(copy)

    coef_copy.wait_send()
    part_copy.wait_send()
    for rel in (0, 1):
        border_wait_send(*ghost_args, rel)
        border_wait_send(*back_args[rel])
    for copy in prod_copies:
        copy.wait_recv()
    result = prod_out[me]
    for step in range(1, n_mesh):
        result = result + prod_in[step - 1]
    reduced_ref[...] = result
    for copy in prod_copies:
        copy.wait_send()


def per_device(coeffs, load, mass, stiffness, edge_ref, conn, ghost_send, order, basis):
    n_mesh = lax.axis_size("mesh")
    block, _, nodes = coeffs.shape
    rows = 3 * block
    ncoef = 2 * block
    elems = conn.shape[1] // 2
    ghosts = ghost_send.shape[1]
    slots = nodes + 2 * ghosts
    basis_count = basis.shape[0]
    share = basis_count // n_mesh
    vmem = pl.BlockSpec(memory_space=pltpu.VMEM)
    anywhere = pl.BlockSpec(memory_space=pl.ANY)
    dma = pltpu.SemaphoreType.DMA

    def body(*refs):
        kernel(n_mesh, *refs)

    resid, reduced = pl.pallas_call(
        body,
        out_shape=(
            jax.ShapeDtypeStruct((rows, nodes), F32),
            jax.ShapeDtypeStruct((share, block), F32),
        ),
        in_specs=[vmem, anywhere, vmem, vmem, vmem, vmem, vmem, vmem, anywhere],
        out_specs=(vmem, vmem),
        scratch_shapes=[
            pltpu.VMEM((rows, nodes), F32),
            pltpu.VMEM((3, basis_count, nodes), BF16),
            pltpu.VMEM((rows, nodes), F32),
            pltpu.VMEM((2 * rows, nodes), BF16),
            pltpu.VMEM((2 * rows, slots), BF16),
            pltpu.VMEM((nodes, 2 * ghosts), BF16),
            pltpu.VMEM((slots, 2 * elems), BF16),
            pltpu.VMEM((rows, 2 * ghosts), F32),
            pltpu.VMEM((2, 2, rows, 2 * ghosts), F32),
            pltpu.VMEM((2 * rows, 2 * ghosts), BF16),
            pltpu.VMEM((2 * rows, 2 * elems), F32),
            pltpu.VMEM((3, 3 * ncoef, 2 * elems), BF16),
            pltpu.VMEM((3, ncoef, 2 * elems), F32),
            pltpu.VMEM((3, 3 * ncoef, 2 * elems), BF16),
            pltpu.VMEM((2, 2 * rows, 2 * elems), BF16),
            pltpu.VMEM((2, rows, 2 * ghosts), F32),
            pltpu.VMEM((2, 2, rows, 2 * ghosts), F32),
            pltpu.VMEM((rows, nodes), F32),
            pltpu.VMEM((rows, nodes), F32),
            pltpu.VMEM((rows, nodes), F32),
            pltpu.VMEM((3, block, nodes), BF16),
            pltpu.VMEM((n_mesh, share, block), F32),
            pltpu.VMEM((n_mesh - 1, share, block), F32),
            dma((2,)),
            dma((2,)),
            dma((2, 2)),
            dma((2, 2)),
            dma((2,)),
            dma((2, 2)),
            dma((2, 2)),
            dma((n_mesh - 1,)),
            dma((n_mesh - 1,)),
        ],
        compiler_params=pltpu.CompilerParams(
            collective_id=0, has_side_effects=True, vmem_limit_bytes=48 * 1024 * 1024
        ),
    )(
        coeffs.transpose(1, 0, 2).reshape(rows, nodes),
        load.transpose(1, 0, 2).reshape(rows, nodes),
        mass.reshape(1, -1),
        stiffness.reshape(1, -1),
        edge_ref.transpose(1, 0, 2),
        conn,
        ghost_send,
        order.reshape(1, -1),
        basis.transpose(1, 0, 2),
    )
    return resid.reshape(3, block, nodes).transpose(1, 0, 2), reduced


def solution(mesh):
    in_specs = (
        P("harm", None, ("case", "mesh")),
        P("harm", None, ("case", "mesh")),
        P("mesh"),
        P("mesh"),
        P(None, None, "mesh"),
        P(None, "mesh"),
        P(None, "mesh"),
        P(),
        P(None, None, "mesh"),
    )
    out_specs = (P("harm", None, ("case", "mesh")), P("mesh", ("case", "harm")))
    return jax.shard_map(
        per_device, mesh=mesh, in_specs=in_specs, out_specs=out_specs, check_vma=False
    )
```

```python
import math

import jax
import jax.numpy as jnp
from jax import lax
from jax.experimental import pallas as pl
from jax.experimental.pallas import tpu as pltpu
from jax.sharding import PartitionSpec as P

OMEGA = 0.1
PRESTRESS = 0.2
F32 = jnp.float32
BF16 = jnp.bfloat16
MESH = pl.DeviceIdType.MESH
LANES = 256


def halves(x):
    high = x.astype(BF16)
    return high, (x - high.astype(F32)).astype(BF16)


def dot(a, b):
    return jnp.dot(a, b, preferred_element_type=F32)


def dot_t(a, b):
    return lax.dot_general(a, b, (((1,), (1,)), ((), ())), preferred_element_type=F32)


def wave(order, samples, ncoef):
    harmonic = (order + 1) // 2
    cosine = (order % 2 == 1) | (order == 0)
    phase = harmonic * samples + jnp.where(cosine, 0, ncoef - ncoef // 4)
    phase = (phase + ncoef // 2) % ncoef - ncoef // 2
    return jnp.cos((2.0 * math.pi / ncoef) * phase.astype(F32))


def in_three(table):
    high, lower = halves(table)
    high = high.astype(F32)
    return jnp.concatenate([high, high, lower.astype(F32)], axis=1).astype(BF16)


def pack_border(full):
    rows, lanes = full.shape
    first = lax.broadcasted_iota(jnp.int32, (rows // 2, lanes), 1) < lanes // 2
    turned = pltpu.roll(full, lanes // 2, 1)
    half = rows // 2
    return (
        jnp.where(first, full[:half], turned[half:]),
        jnp.where(first, turned[:half], full[half:]),
    )


def unpack_border(low_part, high_part):
    half, lanes = low_part.shape
    first = lax.broadcasted_iota(jnp.int32, (half, lanes), 1) < lanes // 2
    top = jnp.where(first, low_part, pltpu.roll(high_part, lanes // 2, 1))
    bottom = jnp.where(first, pltpu.roll(low_part, lanes // 2, 1), high_part)
    return jnp.concatenate([top, bottom], axis=0)


def kernel(
    n_mesh,
    coef_hbm, load_hbm, mass_hbm, stiff_hbm, edge_hbm, conn_hbm, ghost_hbm, order_hbm, basis_hbm,
    resid_ref, reduced_ref,
    coef_ref, load_ref, mass_ref, stiff_ref, edge_ref, conn_ref, ghost_ref, order_ref, basis_ref,
    coef_in, own_hl, other_hl, pick, inc, ghost_out, ghost_in, ghost_hl,
    edge_own, edge_hl, disp, force_hl, coef_hl, back_out, back_in, part_out, part_in, main_own, low,
    prod_out, prod_in,
    local_sem, coef_sem, ghost_send_sem, ghost_recv_sem, part_sem,
    back_send_sem, back_recv_sem, prod_send_sem, prod_recv_sem,
):
    rows, nodes = coef_ref.shape
    block = rows // 3
    ncoef = 2 * block
    ghosts = ghost_ref.shape[1]
    elems = conn_ref.shape[1] // 2
    slots = nodes + 2 * ghosts
    sub = prod_out.shape[1]
    fold = prod_out.shape[2] // block
    share = sub * fold
    me = lax.axis_index("mesh")
    harm = lax.axis_index("harm")
    other = 1 - harm
    has_low, has_up = me > 0, me < n_mesh - 1

    barrier = pltpu.get_barrier_semaphore()
    pl.semaphore_signal(barrier, inc=1, device_id={"harm": other}, device_id_type=MESH)
    for step in range(1, n_mesh):
        pl.semaphore_signal(
            barrier, inc=1, device_id={"mesh": lax.rem(me + step, n_mesh)}, device_id_type=MESH
        )

    @pl.when(has_low)
    def _():
        pl.semaphore_signal(
            barrier, inc=1, device_id={"mesh": me - 1, "harm": other}, device_id_type=MESH
        )

    @pl.when(has_up)
    def _():
        pl.semaphore_signal(
            barrier, inc=1, device_id={"mesh": me + 1, "harm": other}, device_id_type=MESH
        )

    fetch = {}
    for at, (name, src, dst) in enumerate((
        ("coef", coef_hbm, coef_ref), ("ghost", ghost_hbm, ghost_ref), ("conn", conn_hbm, conn_ref),
        ("order", order_hbm, order_ref), ("edge", edge_hbm, edge_ref),
        ("stiff", stiff_hbm, stiff_ref), ("mass", mass_hbm, mass_ref),
        ("load", load_hbm, load_ref), ("basis", basis_hbm, basis_ref),
    )):
        fetch[name] = pltpu.make_async_copy(src, dst, local_sem.at[at])
        fetch[name].start()
    fetch["coef"].wait()
    fetch["ghost"].wait()

    high, lower = halves(coef_ref[...])
    own_hl[0:rows, :] = high
    own_hl[rows : 2 * rows, :] = lower
    shared = jnp.concatenate([ghost_ref[1:2, :], ghost_ref[0:1, :]], axis=1)
    node_ids = lax.broadcasted_iota(jnp.int32, (nodes, 2 * ghosts), 0)
    pick[...] = jnp.where(node_ids == shared, 1.0, 0.0).astype(BF16)
    picked = dot(own_hl[...], pick[...])
    ghost_out[0], ghost_out[1] = pack_border(picked[0:rows] + picked[rows : 2 * rows])

    arrivals = n_mesh + has_low.astype(jnp.int32) + has_up.astype(jnp.int32)
    pl.semaphore_wait(barrier, arrivals)

    coef_copy = pltpu.make_async_remote_copy(
        src_ref=coef_ref, dst_ref=coef_in, send_sem=coef_sem.at[0], recv_sem=coef_sem.at[1],
        device_id={"harm": other}, device_id_type=MESH,
    )
    coef_copy.start()

    def border(src, dst, send_sem, recv_sem, side, rel):
        return pltpu.make_async_remote_copy(
            src_ref=src.at[side], dst_ref=dst.at[side, rel], send_sem=send_sem.at[side, rel],
            recv_sem=recv_sem.at[side, rel],
            device_id={
                "mesh": me + 1 if side == 0 else me - 1, "harm": harm if rel == 0 else other,
            },
            device_id_type=MESH,
        )

    there = (has_up, has_low)
    come = (has_low, has_up)

    def border_start(src, dst, send_sem, recv_sem, rel):
        for side in (0, 1):
            @pl.when(there[side])
            def _():
                border(src, dst, send_sem, recv_sem, side, rel).start()

    def border_wait_recv(src, dst, send_sem, recv_sem, rel):
        for side in (0, 1):
            @pl.when(come[side])
            def _():
                border(src, dst, send_sem, recv_sem, side, rel).wait_recv()

            @pl.when(jnp.logical_not(come[side]))
            def _():
                dst[side, rel] = jnp.zeros(dst.shape[2:], F32)

    def border_wait_send(src, dst, send_sem, recv_sem, rel):
        for side in (0, 1):
            @pl.when(there[side])
            def _():
                border(src, dst, send_sem, recv_sem, side, rel).wait_send()

    ghost_args = (ghost_out, ghost_in, ghost_send_sem, ghost_recv_sem)
    border_start(*ghost_args, 0)
    border_start(*ghost_args, 1)

    fetch["conn"].wait()

    mine = pl.ds(pl.multiple_of(harm * elems, elems), elems)
    step_rows = 64

    def fill(k, _):
        base = pl.multiple_of(k * step_rows, step_rows)
        for at in range(0, elems, LANES):
            cols = pl.ds(pl.multiple_of(harm * elems + at, LANES), LANES)
            ids = lax.broadcasted_iota(jnp.int32, (step_rows, LANES), 0) + base
            first = jnp.where(ids == conn_ref[0:1, cols], 1.0, 0.0)
            second = jnp.where(ids == conn_ref[1:2, cols], 1.0, 0.0)
            third = jnp.where(ids == conn_ref[2:3, cols], 1.0, 0.0)
            inc[pl.ds(base, step_rows), at : at + LANES] = (second - first).astype(BF16)
            inc[pl.ds(base, step_rows), elems + at : elems + at + LANES] = (third - first).astype(BF16)
        return 0

    lax.fori_loop(0, slots // step_rows, fill, 0)

    fetch["order"].wait()
    row = order_ref[...]
    row = jnp.where(harm == 0, row, jnp.concatenate([row[:, block:], row[:, :block]], axis=1))
    lanes = lax.broadcasted_iota(jnp.int32, (ncoef, ncoef), 1)
    subs = lax.broadcasted_iota(jnp.int32, (ncoef, ncoef), 0)
    synth3 = in_three(wave(row, subs, ncoef))
    column = jnp.sum(jnp.where(lanes == subs, row.astype(F32), 0.0), axis=1, keepdims=True)
    column = column.astype(jnp.int32)
    weight = jnp.where((column == 0) | (column == ncoef - 1), 1.0, 2.0) / ncoef
    proj3 = in_three(wave(column, lanes, ncoef) * weight)
    freq = (OMEGA * ((column[0:block] + 1) // 2).astype(F32)) ** 2

    for at in range(0, 2 * elems, LANES):
        edge_own[:, at : at + LANES] = dot(own_hl[...], inc[0:nodes, at : at + LANES])

    coef_copy.wait_recv()
    high, lower = halves(coef_in[...])
    other_hl[0:rows, 0:nodes] = high
    other_hl[rows : 2 * rows, 0:nodes] = lower
    border_wait_recv(*ghost_args, 0)
    border_wait_recv(*ghost_args, 1)
    high, lower = halves(unpack_border(ghost_in[0, 0], ghost_in[1, 0]))
    ghost_hl[0:rows, :] = high
    ghost_hl[rows : 2 * rows, :] = lower
    high, lower = halves(unpack_border(ghost_in[0, 1], ghost_in[1, 1]))
    other_hl[0:rows, nodes:slots] = high
    other_hl[rows : 2 * rows, nodes:slots] = lower

    for at in range(0, 2 * elems, LANES):
        cols = slice(at, at + LANES)
        mine_edges = edge_own[:, cols] + dot(ghost_hl[...], inc[nodes:slots, cols])
        other_edges = dot(other_hl[...], inc[:, cols])
        for half, edges in enumerate((mine_edges, other_edges)):
            high, lower = halves(edges[0:rows] + edges[rows : 2 * rows])
            for c in range(3):
                part = slice(c * block, (c + 1) * block)
                for third, piece in enumerate((high, lower, high)):
                    top = third * ncoef + half * block
                    edge_hl[c, top : top + block, cols] = piece[part]
    for c in range(3):
        for at in range(0, 2 * elems, LANES):
            cols = slice(at, at + LANES)
            disp[c, :, cols] = dot(synth3, edge_hl[c, :, cols])

    fetch["edge"].wait()
    fetch["stiff"].wait()
    def sample_rows(k, _):
        base = pl.multiple_of(k * 16, 16)
        times = pl.ds(base, 16)
        for at in range(0, elems, LANES):
            cols = pl.ds(pl.multiple_of(harm * elems + at, LANES), LANES)
            stiff = stiff_ref[0:1, cols]
            refs_b = [edge_ref[c, 0:1, cols] for c in range(3)]
            refs_c = [edge_ref[c, 1:2, cols] for c in range(3)]
            refs_d = [x - y for x, y in zip(refs_c, refs_b)]

            def pull(stretch, refs):
                rest = refs[0] * refs[0] + refs[1] * refs[1] + refs[2] * refs[2]
                square = stretch[0] * stretch[0] + stretch[1] * stretch[1] + stretch[2] * stretch[2]
                return stiff * (0.5 * (square - rest) + PRESTRESS)

            str_b = [refs_b[c] + disp[c, times, at : at + LANES] for c in range(3)]
            str_c = [refs_c[c] + disp[c, times, elems + at : elems + at + LANES] for c in range(3)]
            str_d = [x - y for x, y in zip(str_c, str_b)]
            ten_b = pull(str_b, refs_b)
            ten_c = pull(str_c, refs_c)
            ten_d = pull(str_d, refs_d)
            for c in range(3):
                mid = ten_d * str_d[c]
                for which, value in enumerate((ten_b * str_b[c] - mid, ten_c * str_c[c] + mid)):
                    high, lower = halves(value)
                    to = slice(which * elems + at, which * elems + at + LANES)
                    force_hl[c, times, to] = high
                    force_hl[c, pl.ds(base + ncoef, 16), to] = lower
                    force_hl[c, pl.ds(base + 2 * ncoef, 16), to] = high
        return 0

    lax.fori_loop(0, ncoef // 16, sample_rows, 0)

    for c in range(3):
        for at in range(0, 2 * elems, LANES):
            cols = slice(at, at + LANES)
            value = dot(proj3, force_hl[c, :, cols])
            high, lower = halves(value)
            for half in (0, 1):
                part = slice(half * block, (half + 1) * block)
                coef_hl[half, c * block : (c + 1) * block, cols] = high[part]
                coef_hl[half, rows + c * block : rows + (c + 1) * block, cols] = lower[part]

    def spread(half, start, stop):
        summed = dot_t(coef_hl[half], inc[start:stop, :])
        return summed[0:rows] + summed[rows : 2 * rows]

    back_args = [
        (back_out.at[rel], back_in, back_send_sem, back_recv_sem, rel) for rel in (0, 1)
    ]
    back_out[1, 1], back_out[1, 0] = pack_border(spread(1, nodes, slots))
    border_start(*back_args[1])
    back_out[0, 1], back_out[0, 0] = pack_border(spread(0, nodes, slots))
    border_start(*back_args[0])
    for at in range(0, nodes, LANES):
        part_out[:, at : at + LANES] = spread(1, at, at + LANES)
    part_copy = pltpu.make_async_remote_copy(
        src_ref=part_out, dst_ref=part_in, send_sem=part_sem.at[0], recv_sem=part_sem.at[1],
        device_id={"harm": other}, device_id_type=MESH,
    )
    part_copy.start()
    fetch["load"].wait()
    fetch["mass"].wait()
    for at in range(0, nodes, LANES):
        cols = slice(at, at + LANES)
        main_own[:, cols] = spread(0, at, at + LANES)

    border_wait_recv(*back_args[0])
    border_wait_recv(*back_args[1])
    back = unpack_border(back_in[1, 0] + back_in[1, 1], back_in[0, 0] + back_in[0, 1])
    high, lower = halves(back)
    ghost_hl[0:rows, :] = high
    ghost_hl[rows : 2 * rows, :] = lower
    part_copy.wait_recv()
    for at in range(0, nodes, LANES):
        cols = slice(at, at + LANES)
        added = dot_t(ghost_hl[...], pick[at : at + LANES, :])
        forces = main_own[:, cols] + part_in[:, cols] + (added[0:rows] + added[rows : 2 * rows])
        for c in range(3):
            part = slice(c * block, (c + 1) * block)
            inertia = freq * mass_ref[0:1, cols] * coef_ref[part, cols]
            value = forces[part] - inertia - load_ref[part, cols]
            resid_ref[part, cols] = value
            low[c, :, cols] = value.astype(BF16)

    fetch["basis"].wait()
    total = None
    for c in range(3):
        term = dot_t(basis_ref[c], low[c])
        total = term if total is None else total + term
    for piece in range(n_mesh):
        prod_out[piece] = jnp.concatenate(
            [total[piece * share + q * sub : piece * share + (q + 1) * sub] for q in range(fold)], axis=1
        )

    prod_copies = []
    for step in range(1, n_mesh):
        peer = lax.rem(me + step, n_mesh)
        copy = pltpu.make_async_remote_copy(
            src_ref=prod_out.at[peer], dst_ref=prod_in.at[step - 1],
            send_sem=prod_send_sem.at[step - 1], recv_sem=prod_recv_sem.at[step - 1],
            device_id={"mesh": peer}, device_id_type=MESH,
        )
        copy.start()
        prod_copies.append(copy)

    coef_copy.wait_send()
    part_copy.wait_send()
    for rel in (0, 1):
        border_wait_send(*ghost_args, rel)
        border_wait_send(*back_args[rel])
    for copy in prod_copies:
        copy.wait_recv()
    result = prod_out[me]
    for step in range(1, n_mesh):
        result = result + prod_in[step - 1]
    for q in range(fold):
        reduced_ref[q * sub : (q + 1) * sub, :] = result[:, q * block : (q + 1) * block]
    for copy in prod_copies:
        copy.wait_send()


def per_device(coeffs, load, mass, stiffness, edge_ref, conn, ghost_send, order, basis):
    n_mesh = lax.axis_size("mesh")
    block, _, nodes = coeffs.shape
    rows = 3 * block
    ncoef = 2 * block
    elems = conn.shape[1] // 2
    ghosts = ghost_send.shape[1]
    slots = nodes + 2 * ghosts
    basis_count = basis.shape[0]
    share = basis_count // n_mesh
    fold = min(128 // block, share)
    vmem = pl.BlockSpec(memory_space=pltpu.VMEM)
    hbm = pl.BlockSpec(memory_space=pltpu.HBM)
    dma = pltpu.SemaphoreType.DMA

    def body(*refs):
        kernel(n_mesh, *refs)

    resid, reduced = pl.pallas_call(
        body,
        out_shape=(
            jax.ShapeDtypeStruct((rows, nodes), F32),
            jax.ShapeDtypeStruct((share, block), F32),
        ),
        in_specs=[hbm] * 9,
        out_specs=(vmem, vmem),
        scratch_shapes=[
            pltpu.VMEM((rows, nodes), F32),
            pltpu.VMEM((rows, nodes), F32),
            pltpu.VMEM((1, nodes), F32),
            pltpu.VMEM((1, 2 * elems), F32),
            pltpu.VMEM((3, 2, 2 * elems), F32),
            pltpu.VMEM((3, 2 * elems), jnp.int32),
            pltpu.VMEM((2, ghosts), jnp.int32),
            pltpu.VMEM((1, ncoef), jnp.int32),
            pltpu.VMEM((3, basis_count, nodes), BF16),
            pltpu.VMEM((rows, nodes), F32),
            pltpu.VMEM((2 * rows, nodes), BF16),
            pltpu.VMEM((2 * rows, slots), BF16),
            pltpu.VMEM((nodes, 2 * ghosts), BF16),
            pltpu.VMEM((slots, 2 * elems), BF16),
            pltpu.VMEM((2, rows // 2, 2 * ghosts), F32),
            pltpu.VMEM((2, 2, rows // 2, 2 * ghosts), F32),
            pltpu.VMEM((2 * rows, 2 * ghosts), BF16),
            pltpu.VMEM((2 * rows, 2 * elems), F32),
            pltpu.VMEM((3, 3 * ncoef, 2 * elems), BF16),
            pltpu.VMEM((3, ncoef, 2 * elems), F32),
            pltpu.VMEM((3, 3 * ncoef, 2 * elems), BF16),
            pltpu.VMEM((2, 2 * rows, 2 * elems), BF16),
            pltpu.VMEM((2, 2, rows // 2, 2 * ghosts), F32),
            pltpu.VMEM((2, 2, rows // 2, 2 * ghosts), F32),
            pltpu.VMEM((rows, nodes), F32),
            pltpu.VMEM((rows, nodes), F32),
            pltpu.VMEM((rows, nodes), F32),
            pltpu.VMEM((3, block, nodes), BF16),
            pltpu.VMEM((n_mesh, share // fold, fold * block), F32),
            pltpu.VMEM((n_mesh - 1, share // fold, fold * block), F32),
            dma((9,)),
            dma((2,)),
            dma((2, 2)),
            dma((2, 2)),
            dma((2,)),
            dma((2, 2)),
            dma((2, 2)),
            dma((n_mesh - 1,)),
            dma((n_mesh - 1,)),
        ],
        compiler_params=pltpu.CompilerParams(
            collective_id=0, has_side_effects=True, vmem_limit_bytes=60 * 1024 * 1024
        ),
    )(
        coeffs.transpose(1, 0, 2).reshape(rows, nodes),
        load.transpose(1, 0, 2).reshape(rows, nodes),
        mass.reshape(1, -1),
        stiffness.reshape(1, -1),
        edge_ref.transpose(1, 0, 2),
        conn,
        ghost_send,
        order.reshape(1, -1),
        basis.transpose(1, 0, 2),
    )
    return resid.reshape(3, block, nodes).transpose(1, 0, 2), reduced


def solution(mesh):
    in_specs = (
        P("harm", None, ("case", "mesh")),
        P("harm", None, ("case", "mesh")),
        P("mesh"),
        P("mesh"),
        P(None, None, "mesh"),
        P(None, "mesh"),
        P(None, "mesh"),
        P(),
        P(None, None, "mesh"),
    )
    out_specs = (P("harm", None, ("case", "mesh")), P("mesh", ("case", "harm")))
    return jax.shard_map(
        per_device, mesh=mesh, in_specs=in_specs, out_specs=out_specs, check_vma=False
    )
```

```python
import math

import jax
import jax.numpy as jnp
from jax import lax
from jax.experimental import pallas as pl
from jax.experimental.pallas import tpu as pltpu
from jax.sharding import PartitionSpec as P

OMEGA = 0.1
PRESTRESS = 0.2
F32 = jnp.float32
BF16 = jnp.bfloat16
MESH = pl.DeviceIdType.MESH
LANES = 256


def halves(x):
    high = x.astype(BF16)
    return high, (x - high.astype(F32)).astype(BF16)


def dot(a, b):
    return jnp.dot(a, b, preferred_element_type=F32)


def dot_t(a, b):
    return lax.dot_general(a, b, (((1,), (1,)), ((), ())), preferred_element_type=F32)


def wave(order, samples, ncoef):
    harmonic = (order + 1) // 2
    cosine = (order % 2 == 1) | (order == 0)
    phase = harmonic * samples + jnp.where(cosine, 0, ncoef - ncoef // 4)
    phase = (phase + ncoef // 2) % ncoef - ncoef // 2
    return jnp.cos((2.0 * math.pi / ncoef) * phase.astype(F32))


def in_three(table):
    high, lower = halves(table)
    high = high.astype(F32)
    return jnp.concatenate([high, high, lower.astype(F32)], axis=1).astype(BF16)


def pack_border(full):
    rows, lanes = full.shape
    first = lax.broadcasted_iota(jnp.int32, (rows // 2, lanes), 1) < lanes // 2
    turned = pltpu.roll(full, lanes // 2, 1)
    half = rows // 2
    return (
        jnp.where(first, full[:half], turned[half:]),
        jnp.where(first, turned[:half], full[half:]),
    )


def unpack_border(low_part, high_part):
    half, lanes = low_part.shape
    first = lax.broadcasted_iota(jnp.int32, (half, lanes), 1) < lanes // 2
    top = jnp.where(first, low_part, pltpu.roll(high_part, lanes // 2, 1))
    bottom = jnp.where(first, pltpu.roll(low_part, lanes // 2, 1), high_part)
    return jnp.concatenate([top, bottom], axis=0)


def kernel(
    n_mesh,
    coef_hbm, load_hbm, mass_hbm, stiff_hbm, edge_hbm, conn_hbm, ghost_hbm, order_hbm, basis_hbm,
    resid_ref, reduced_ref,
    coef_ref, load_ref, mass_ref, stiff_ref, edge_ref, conn_ref, ghost_ref, order_ref, basis_ref,
    coef_in, own_hl, other_hl, pick, inc, ghost_out, ghost_in, ghost_hl,
    edge_own, edge_hl, disp, force_hl, coef_hl, back_out, back_in, part_out, part_in, main_own, low,
    prod_out, prod_in,
    local_sem, coef_sem, ghost_send_sem, ghost_recv_sem, part_sem,
    back_send_sem, back_recv_sem, prod_send_sem, prod_recv_sem, reach_sem,
):
    rows, nodes = coef_ref.shape
    block = rows // 3
    ncoef = 2 * block
    ghosts = ghost_ref.shape[1]
    elems = conn_ref.shape[1] // 2
    slots = nodes + 2 * ghosts
    sub = prod_out.shape[1]
    fold = prod_out.shape[2] // block
    share = sub * fold
    me = lax.axis_index("mesh")
    harm = lax.axis_index("harm")
    other = 1 - harm
    has_low, has_up = me > 0, me < n_mesh - 1

    barrier = pltpu.get_barrier_semaphore()
    pl.semaphore_signal(barrier, inc=1, device_id={"harm": other}, device_id_type=MESH)
    for side_ok, to in ((has_low, me - 1), (has_up, me + 1)):
        @pl.when(side_ok)
        def _():
            for core in (harm, other):
                pl.semaphore_signal(
                    barrier, inc=1, device_id={"mesh": to, "harm": core}, device_id_type=MESH
                )

    fetch = {}
    for at, (name, src, dst) in enumerate((
        ("coef", coef_hbm, coef_ref), ("ghost", ghost_hbm, ghost_ref), ("conn", conn_hbm, conn_ref),
        ("order", order_hbm, order_ref), ("edge", edge_hbm, edge_ref),
        ("stiff", stiff_hbm, stiff_ref), ("mass", mass_hbm, mass_ref),
        ("load", load_hbm, load_ref), ("basis", basis_hbm, basis_ref),
    )):
        fetch[name] = pltpu.make_async_copy(src, dst, local_sem.at[at])
        fetch[name].start()
    fetch["coef"].wait()
    fetch["ghost"].wait()

    high, lower = halves(coef_ref[...])
    own_hl[0:rows, :] = high
    own_hl[rows : 2 * rows, :] = lower
    shared = jnp.concatenate([ghost_ref[1:2, :], ghost_ref[0:1, :]], axis=1)
    node_ids = lax.broadcasted_iota(jnp.int32, (nodes, 2 * ghosts), 0)
    pick[...] = jnp.where(node_ids == shared, 1.0, 0.0).astype(BF16)
    picked = dot(own_hl[...], pick[...])
    ghost_out[0], ghost_out[1] = pack_border(picked[0:rows] + picked[rows : 2 * rows])

    arrivals = 1 + 2 * (has_low.astype(jnp.int32) + has_up.astype(jnp.int32))
    pl.semaphore_wait(barrier, arrivals)

    coef_copy = pltpu.make_async_remote_copy(
        src_ref=coef_ref, dst_ref=coef_in, send_sem=coef_sem.at[0], recv_sem=coef_sem.at[1],
        device_id={"harm": other}, device_id_type=MESH,
    )
    coef_copy.start()

    def border(src, dst, send_sem, recv_sem, side, rel):
        return pltpu.make_async_remote_copy(
            src_ref=src.at[side], dst_ref=dst.at[side, rel], send_sem=send_sem.at[side, rel],
            recv_sem=recv_sem.at[side, rel],
            device_id={
                "mesh": me + 1 if side == 0 else me - 1, "harm": harm if rel == 0 else other,
            },
            device_id_type=MESH,
        )

    reaches = []
    while 2 << len(reaches) < n_mesh:
        reaches.append(2 << len(reaches))

    def tell(at):
        reach = reaches[at]
        for ok, to in ((me >= reach, me - reach), (me + reach < n_mesh, me + reach)):
            @pl.when(ok)
            def _():
                pl.semaphore_signal(
                    reach_sem.at[at], inc=1, device_id={"mesh": to}, device_id_type=MESH
                )

    def hear(at):
        reach = reaches[at]
        count = (me >= reach).astype(jnp.int32) + (me + reach < n_mesh).astype(jnp.int32)

        @pl.when(count > 0)
        def _():
            pl.semaphore_wait(reach_sem.at[at], count)

    there = (has_up, has_low)
    come = (has_low, has_up)

    def border_start(src, dst, send_sem, recv_sem, rel):
        for side in (0, 1):
            @pl.when(there[side])
            def _():
                border(src, dst, send_sem, recv_sem, side, rel).start()

    def border_wait_recv(src, dst, send_sem, recv_sem, rel):
        for side in (0, 1):
            @pl.when(come[side])
            def _():
                border(src, dst, send_sem, recv_sem, side, rel).wait_recv()

            @pl.when(jnp.logical_not(come[side]))
            def _():
                dst[side, rel] = jnp.zeros(dst.shape[2:], F32)

    def border_wait_send(src, dst, send_sem, recv_sem, rel):
        for side in (0, 1):
            @pl.when(there[side])
            def _():
                border(src, dst, send_sem, recv_sem, side, rel).wait_send()

    ghost_args = (ghost_out, ghost_in, ghost_send_sem, ghost_recv_sem)
    border_start(*ghost_args, 0)
    border_start(*ghost_args, 1)

    fetch["conn"].wait()

    mine = pl.ds(pl.multiple_of(harm * elems, elems), elems)
    step_rows = 64

    def fill(k, _):
        base = pl.multiple_of(k * step_rows, step_rows)
        for at in range(0, elems, LANES):
            cols = pl.ds(pl.multiple_of(harm * elems + at, LANES), LANES)
            ids = lax.broadcasted_iota(jnp.int32, (step_rows, LANES), 0) + base
            first = jnp.where(ids == conn_ref[0:1, cols], 1.0, 0.0)
            second = jnp.where(ids == conn_ref[1:2, cols], 1.0, 0.0)
            third = jnp.where(ids == conn_ref[2:3, cols], 1.0, 0.0)
            inc[pl.ds(base, step_rows), at : at + LANES] = (second - first).astype(BF16)
            inc[pl.ds(base, step_rows), elems + at : elems + at + LANES] = (third - first).astype(BF16)
        return 0

    lax.fori_loop(0, slots // step_rows, fill, 0)

    fetch["order"].wait()
    row = order_ref[...]
    row = jnp.where(harm == 0, row, jnp.concatenate([row[:, block:], row[:, :block]], axis=1))
    lanes = lax.broadcasted_iota(jnp.int32, (ncoef, ncoef), 1)
    subs = lax.broadcasted_iota(jnp.int32, (ncoef, ncoef), 0)
    synth3 = in_three(wave(row, subs, ncoef))
    column = jnp.sum(jnp.where(lanes == subs, row.astype(F32), 0.0), axis=1, keepdims=True)
    column = column.astype(jnp.int32)
    weight = jnp.where((column == 0) | (column == ncoef - 1), 1.0, 2.0) / ncoef
    proj3 = in_three(wave(column, lanes, ncoef) * weight)
    freq = (OMEGA * ((column[0:block] + 1) // 2).astype(F32)) ** 2

    for at in range(0, 2 * elems, LANES):
        edge_own[:, at : at + LANES] = dot(own_hl[...], inc[0:nodes, at : at + LANES])

    coef_copy.wait_recv()
    high, lower = halves(coef_in[...])
    other_hl[0:rows, 0:nodes] = high
    other_hl[rows : 2 * rows, 0:nodes] = lower
    border_wait_recv(*ghost_args, 0)
    border_wait_recv(*ghost_args, 1)
    if reaches:
        tell(0)
    high, lower = halves(unpack_border(ghost_in[0, 0], ghost_in[1, 0]))
    ghost_hl[0:rows, :] = high
    ghost_hl[rows : 2 * rows, :] = lower
    high, lower = halves(unpack_border(ghost_in[0, 1], ghost_in[1, 1]))
    other_hl[0:rows, nodes:slots] = high
    other_hl[rows : 2 * rows, nodes:slots] = lower

    for at in range(0, 2 * elems, LANES):
        cols = slice(at, at + LANES)
        mine_edges = edge_own[:, cols] + dot(ghost_hl[...], inc[nodes:slots, cols])
        other_edges = dot(other_hl[...], inc[:, cols])
        for half, edges in enumerate((mine_edges, other_edges)):
            high, lower = halves(edges[0:rows] + edges[rows : 2 * rows])
            for c in range(3):
                part = slice(c * block, (c + 1) * block)
                for third, piece in enumerate((high, lower, high)):
                    top = third * ncoef + half * block
                    edge_hl[c, top : top + block, cols] = piece[part]
    for c in range(3):
        for at in range(0, 2 * elems, LANES):
            cols = slice(at, at + LANES)
            disp[c, :, cols] = dot(synth3, edge_hl[c, :, cols])

    if reaches:
        hear(0)
    for at in range(1, min(2, len(reaches))):
        tell(at)

    fetch["edge"].wait()
    fetch["stiff"].wait()
    def sample_rows(k, _):
        base = pl.multiple_of(k * 16, 16)
        times = pl.ds(base, 16)
        for at in range(0, elems, LANES):
            cols = pl.ds(pl.multiple_of(harm * elems + at, LANES), LANES)
            stiff = stiff_ref[0:1, cols]
            refs_b = [edge_ref[c, 0:1, cols] for c in range(3)]
            refs_c = [edge_ref[c, 1:2, cols] for c in range(3)]
            refs_d = [x - y for x, y in zip(refs_c, refs_b)]

            def pull(stretch, refs):
                rest = refs[0] * refs[0] + refs[1] * refs[1] + refs[2] * refs[2]
                square = stretch[0] * stretch[0] + stretch[1] * stretch[1] + stretch[2] * stretch[2]
                return stiff * (0.5 * (square - rest) + PRESTRESS)

            str_b = [refs_b[c] + disp[c, times, at : at + LANES] for c in range(3)]
            str_c = [refs_c[c] + disp[c, times, elems + at : elems + at + LANES] for c in range(3)]
            str_d = [x - y for x, y in zip(str_c, str_b)]
            ten_b = pull(str_b, refs_b)
            ten_c = pull(str_c, refs_c)
            ten_d = pull(str_d, refs_d)
            for c in range(3):
                mid = ten_d * str_d[c]
                for which, value in enumerate((ten_b * str_b[c] - mid, ten_c * str_c[c] + mid)):
                    high, lower = halves(value)
                    to = slice(which * elems + at, which * elems + at + LANES)
                    force_hl[c, times, to] = high
                    force_hl[c, pl.ds(base + ncoef, 16), to] = lower
                    force_hl[c, pl.ds(base + 2 * ncoef, 16), to] = high
        return 0

    lax.fori_loop(0, ncoef // 16, sample_rows, 0)

    for c in range(3):
        for at in range(0, 2 * elems, LANES):
            cols = slice(at, at + LANES)
            value = dot(proj3, force_hl[c, :, cols])
            high, lower = halves(value)
            for half in (0, 1):
                part = slice(half * block, (half + 1) * block)
                coef_hl[half, c * block : (c + 1) * block, cols] = high[part]
                coef_hl[half, rows + c * block : rows + (c + 1) * block, cols] = lower[part]

    def spread(half, start, stop):
        summed = dot_t(coef_hl[half], inc[start:stop, :])
        return summed[0:rows] + summed[rows : 2 * rows]

    back_args = [
        (back_out.at[rel], back_in, back_send_sem, back_recv_sem, rel) for rel in (0, 1)
    ]
    back_out[1, 1], back_out[1, 0] = pack_border(spread(1, nodes, slots))
    border_start(*back_args[1])
    back_out[0, 1], back_out[0, 0] = pack_border(spread(0, nodes, slots))
    border_start(*back_args[0])
    for at in range(0, nodes, LANES):
        part_out[:, at : at + LANES] = spread(1, at, at + LANES)
    part_copy = pltpu.make_async_remote_copy(
        src_ref=part_out, dst_ref=part_in, send_sem=part_sem.at[0], recv_sem=part_sem.at[1],
        device_id={"harm": other}, device_id_type=MESH,
    )
    part_copy.start()
    fetch["load"].wait()
    fetch["mass"].wait()
    for at in range(0, nodes, LANES):
        cols = slice(at, at + LANES)
        main_own[:, cols] = spread(0, at, at + LANES)

    border_wait_recv(*back_args[0])
    border_wait_recv(*back_args[1])
    back = unpack_border(back_in[1, 0] + back_in[1, 1], back_in[0, 0] + back_in[0, 1])
    high, lower = halves(back)
    ghost_hl[0:rows, :] = high
    ghost_hl[rows : 2 * rows, :] = lower
    part_copy.wait_recv()
    for at in range(0, nodes, LANES):
        cols = slice(at, at + LANES)
        added = dot_t(ghost_hl[...], pick[at : at + LANES, :])
        forces = main_own[:, cols] + part_in[:, cols] + (added[0:rows] + added[rows : 2 * rows])
        for c in range(3):
            part = slice(c * block, (c + 1) * block)
            inertia = freq * mass_ref[0:1, cols] * coef_ref[part, cols]
            value = forces[part] - inertia - load_ref[part, cols]
            resid_ref[part, cols] = value
            low[c, :, cols] = value.astype(BF16)

    fetch["basis"].wait()
    total = None
    for c in range(3):
        term = dot_t(basis_ref[c], low[c])
        total = term if total is None else total + term
    for piece in range(n_mesh):
        prod_out[piece] = jnp.concatenate(
            [total[piece * share + q * sub : piece * share + (q + 1) * sub] for q in range(fold)], axis=1
        )

    for at in range(1, len(reaches)):
        hear(at)
        if at + 1 < len(reaches):
            tell(at + 1)
    prod_copies = []
    for step in range(1, n_mesh):
        peer = lax.rem(me + step, n_mesh)
        copy = pltpu.make_async_remote_copy(
            src_ref=prod_out.at[peer], dst_ref=prod_in.at[step - 1],
            send_sem=prod_send_sem.at[step - 1], recv_sem=prod_recv_sem.at[step - 1],
            device_id={"mesh": peer}, device_id_type=MESH,
        )
        copy.start()
        prod_copies.append(copy)

    coef_copy.wait_send()
    part_copy.wait_send()
    for rel in (0, 1):
        border_wait_send(*ghost_args, rel)
        border_wait_send(*back_args[rel])
    for copy in prod_copies:
        copy.wait_recv()
    result = prod_out[me]
    for step in range(1, n_mesh):
        result = result + prod_in[step - 1]
    for q in range(fold):
        reduced_ref[q * sub : (q + 1) * sub, :] = result[:, q * block : (q + 1) * block]
    for copy in prod_copies:
        copy.wait_send()


def per_device(coeffs, load, mass, stiffness, edge_ref, conn, ghost_send, order, basis):
    n_mesh = lax.axis_size("mesh")
    block, _, nodes = coeffs.shape
    rows = 3 * block
    ncoef = 2 * block
    elems = conn.shape[1] // 2
    ghosts = ghost_send.shape[1]
    slots = nodes + 2 * ghosts
    basis_count = basis.shape[0]
    share = basis_count // n_mesh
    fold = min(128 // block, share)
    vmem = pl.BlockSpec(memory_space=pltpu.VMEM)
    hbm = pl.BlockSpec(memory_space=pltpu.HBM)
    dma = pltpu.SemaphoreType.DMA

    def body(*refs):
        kernel(n_mesh, *refs)

    resid, reduced = pl.pallas_call(
        body,
        out_shape=(
            jax.ShapeDtypeStruct((rows, nodes), F32),
            jax.ShapeDtypeStruct((share, block), F32),
        ),
        in_specs=[hbm] * 9,
        out_specs=(vmem, vmem),
        scratch_shapes=[
            pltpu.VMEM((rows, nodes), F32),
            pltpu.VMEM((rows, nodes), F32),
            pltpu.VMEM((1, nodes), F32),
            pltpu.VMEM((1, 2 * elems), F32),
            pltpu.VMEM((3, 2, 2 * elems), F32),
            pltpu.VMEM((3, 2 * elems), jnp.int32),
            pltpu.VMEM((2, ghosts), jnp.int32),
            pltpu.VMEM((1, ncoef), jnp.int32),
            pltpu.VMEM((3, basis_count, nodes), BF16),
            pltpu.VMEM((rows, nodes), F32),
            pltpu.VMEM((2 * rows, nodes), BF16),
            pltpu.VMEM((2 * rows, slots), BF16),
            pltpu.VMEM((nodes, 2 * ghosts), BF16),
            pltpu.VMEM((slots, 2 * elems), BF16),
            pltpu.VMEM((2, rows // 2, 2 * ghosts), F32),
            pltpu.VMEM((2, 2, rows // 2, 2 * ghosts), F32),
            pltpu.VMEM((2 * rows, 2 * ghosts), BF16),
            pltpu.VMEM((2 * rows, 2 * elems), F32),
            pltpu.VMEM((3, 3 * ncoef, 2 * elems), BF16),
            pltpu.VMEM((3, ncoef, 2 * elems), F32),
            pltpu.VMEM((3, 3 * ncoef, 2 * elems), BF16),
            pltpu.VMEM((2, 2 * rows, 2 * elems), BF16),
            pltpu.VMEM((2, 2, rows // 2, 2 * ghosts), F32),
            pltpu.VMEM((2, 2, rows // 2, 2 * ghosts), F32),
            pltpu.VMEM((rows, nodes), F32),
            pltpu.VMEM((rows, nodes), F32),
            pltpu.VMEM((rows, nodes), F32),
            pltpu.VMEM((3, block, nodes), BF16),
            pltpu.VMEM((n_mesh, share // fold, fold * block), F32),
            pltpu.VMEM((n_mesh - 1, share // fold, fold * block), F32),
            dma((9,)),
            dma((2,)),
            dma((2, 2)),
            dma((2, 2)),
            dma((2,)),
            dma((2, 2)),
            dma((2, 2)),
            dma((n_mesh - 1,)),
            dma((n_mesh - 1,)),
            pltpu.SemaphoreType.REGULAR((8,)),
        ],
        compiler_params=pltpu.CompilerParams(
            collective_id=0, has_side_effects=True, vmem_limit_bytes=60 * 1024 * 1024
        ),
    )(
        coeffs.transpose(1, 0, 2).reshape(rows, nodes),
        load.transpose(1, 0, 2).reshape(rows, nodes),
        mass.reshape(1, -1),
        stiffness.reshape(1, -1),
        edge_ref.transpose(1, 0, 2),
        conn,
        ghost_send,
        order.reshape(1, -1),
        basis.transpose(1, 0, 2),
    )
    return resid.reshape(3, block, nodes).transpose(1, 0, 2), reduced


def solution(mesh):
    in_specs = (
        P("harm", None, ("case", "mesh")),
        P("harm", None, ("case", "mesh")),
        P("mesh"),
        P("mesh"),
        P(None, None, "mesh"),
        P(None, "mesh"),
        P(None, "mesh"),
        P(),
        P(None, None, "mesh"),
    )
    out_specs = (P("harm", None, ("case", "mesh")), P("mesh", ("case", "harm")))
    return jax.shard_map(
        per_device, mesh=mesh, in_specs=in_specs, out_specs=out_specs, check_vma=False
    )
```

```python
import math

import jax
import jax.numpy as jnp
from jax import lax
from jax.experimental import pallas as pl
from jax.experimental.pallas import tpu as pltpu
from jax.sharding import PartitionSpec as P

OMEGA = 0.1
PRESTRESS = 0.2
F32 = jnp.float32
BF16 = jnp.bfloat16
MESH = pl.DeviceIdType.MESH
LANES = 256


def halves(x):
    high = x.astype(BF16)
    return high, (x - high.astype(F32)).astype(BF16)


def dot(a, b):
    return jnp.dot(a, b, preferred_element_type=F32)


def dot_t(a, b):
    return lax.dot_general(a, b, (((1,), (1,)), ((), ())), preferred_element_type=F32)


def wave(order, samples, ncoef):
    harmonic = (order + 1) // 2
    cosine = (order % 2 == 1) | (order == 0)
    phase = harmonic * samples + jnp.where(cosine, 0, ncoef - ncoef // 4)
    phase = (phase + ncoef // 2) % ncoef - ncoef // 2
    return jnp.cos((2.0 * math.pi / ncoef) * phase.astype(F32))


def in_three(table):
    high, lower = halves(table)
    high = high.astype(F32)
    return jnp.concatenate([high, high, lower.astype(F32)], axis=1).astype(BF16)


def pack_border(full):
    rows, lanes = full.shape
    first = lax.broadcasted_iota(jnp.int32, (rows // 2, lanes), 1) < lanes // 2
    turned = pltpu.roll(full, lanes // 2, 1)
    half = rows // 2
    return (
        jnp.where(first, full[:half], turned[half:]),
        jnp.where(first, turned[:half], full[half:]),
    )


def unpack_border(low_part, high_part):
    half, lanes = low_part.shape
    first = lax.broadcasted_iota(jnp.int32, (half, lanes), 1) < lanes // 2
    top = jnp.where(first, low_part, pltpu.roll(high_part, lanes // 2, 1))
    bottom = jnp.where(first, pltpu.roll(low_part, lanes // 2, 1), high_part)
    return jnp.concatenate([top, bottom], axis=0)


def kernel(
    n_mesh,
    coef_hbm, load_hbm, mass_hbm, stiff_hbm, edge_hbm, conn_hbm, ghost_hbm, order_hbm, basis_hbm,
    resid_ref, reduced_ref,
    coef_ref, load_ref, mass_ref, stiff_ref, edge_ref, conn_ref, ghost_ref, order_ref, basis_ref,
    coef_in, own_hl, other_hl, pick, inc, ghost_out, ghost_in, ghost_hl,
    edge_own, edge_hl, disp, force_hl, coef_hl, back_out, back_in, part_out, part_in, main_own, low,
    prod_out, prod_in,
    local_sem, coef_sem, ghost_send_sem, ghost_recv_sem, part_sem,
    back_send_sem, back_recv_sem, prod_send_sem, prod_recv_sem,
):
    rows, nodes = coef_ref.shape
    block = rows // 3
    ncoef = 2 * block
    ghosts = ghost_ref.shape[1]
    elems = conn_ref.shape[1] // 2
    slots = nodes + 2 * ghosts
    sub = prod_out.shape[1]
    fold = prod_out.shape[2] // block
    share = sub * fold
    me = lax.axis_index("mesh")
    harm = lax.axis_index("harm")
    other = 1 - harm
    has_low, has_up = me > 0, me < n_mesh - 1

    barrier = pltpu.get_barrier_semaphore()
    pl.semaphore_signal(barrier, inc=1, device_id={"harm": other}, device_id_type=MESH)
    for step in range(1, n_mesh):
        pl.semaphore_signal(
            barrier, inc=1, device_id={"mesh": lax.rem(me + step, n_mesh)}, device_id_type=MESH
        )

    @pl.when(has_low)
    def _():
        pl.semaphore_signal(
            barrier, inc=1, device_id={"mesh": me - 1, "harm": other}, device_id_type=MESH
        )

    @pl.when(has_up)
    def _():
        pl.semaphore_signal(
            barrier, inc=1, device_id={"mesh": me + 1, "harm": other}, device_id_type=MESH
        )

    fetch = {}
    for at, (name, src, dst) in enumerate((
        ("coef", coef_hbm, coef_ref), ("ghost", ghost_hbm, ghost_ref), ("conn", conn_hbm, conn_ref),
        ("order", order_hbm, order_ref), ("edge", edge_hbm, edge_ref),
        ("stiff", stiff_hbm, stiff_ref), ("mass", mass_hbm, mass_ref),
        ("load", load_hbm, load_ref), ("basis", basis_hbm, basis_ref),
    )):
        fetch[name] = pltpu.make_async_copy(src, dst, local_sem.at[at])
        fetch[name].start()
    fetch["coef"].wait()
    fetch["ghost"].wait()

    high, lower = halves(coef_ref[...])
    own_hl[0:rows, :] = high
    own_hl[rows : 2 * rows, :] = lower
    shared = jnp.concatenate([ghost_ref[1:2, :], ghost_ref[0:1, :]], axis=1)
    node_ids = lax.broadcasted_iota(jnp.int32, (nodes, 2 * ghosts), 0)
    pick[...] = jnp.where(node_ids == shared, 1.0, 0.0).astype(BF16)
    picked = dot(own_hl[...], pick[...])
    ghost_out[0], ghost_out[1] = pack_border(picked[0:rows] + picked[rows : 2 * rows])

    arrivals = n_mesh + has_low.astype(jnp.int32) + has_up.astype(jnp.int32)
    pl.semaphore_wait(barrier, arrivals)

    coef_copy = pltpu.make_async_remote_copy(
        src_ref=coef_ref, dst_ref=coef_in, send_sem=coef_sem.at[0], recv_sem=coef_sem.at[1],
        device_id={"harm": other}, device_id_type=MESH,
    )
    coef_copy.start()

    def border(src, dst, send_sem, recv_sem, side, rel):
        return pltpu.make_async_remote_copy(
            src_ref=src.at[side], dst_ref=dst.at[side, rel], send_sem=send_sem.at[side, rel],
            recv_sem=recv_sem.at[side, rel],
            device_id={
                "mesh": me + 1 if side == 0 else me - 1, "harm": harm if rel == 0 else other,
            },
            device_id_type=MESH,
        )

    there = (has_up, has_low)
    come = (has_low, has_up)

    def border_start(src, dst, send_sem, recv_sem, rel):
        for side in (0, 1):
            @pl.when(there[side])
            def _():
                border(src, dst, send_sem, recv_sem, side, rel).start()

    def border_wait_recv(src, dst, send_sem, recv_sem, rel):
        for side in (0, 1):
            @pl.when(come[side])
            def _():
                border(src, dst, send_sem, recv_sem, side, rel).wait_recv()

            @pl.when(jnp.logical_not(come[side]))
            def _():
                dst[side, rel] = jnp.zeros(dst.shape[2:], F32)

    def border_wait_send(src, dst, send_sem, recv_sem, rel):
        for side in (0, 1):
            @pl.when(there[side])
            def _():
                border(src, dst, send_sem, recv_sem, side, rel).wait_send()

    ghost_args = (ghost_out, ghost_in, ghost_send_sem, ghost_recv_sem)
    border_start(*ghost_args, 0)
    border_start(*ghost_args, 1)

    fetch["conn"].wait()

    mine = pl.ds(pl.multiple_of(harm * elems, elems), elems)
    step_rows = 64

    def fill(k, _):
        base = pl.multiple_of(k * step_rows, step_rows)
        for at in range(0, elems, LANES):
            cols = pl.ds(pl.multiple_of(harm * elems + at, LANES), LANES)
            ids = lax.broadcasted_iota(jnp.int32, (step_rows, LANES), 0) + base
            first = jnp.where(ids == conn_ref[0:1, cols], 1.0, 0.0)
            second = jnp.where(ids == conn_ref[1:2, cols], 1.0, 0.0)
            third = jnp.where(ids == conn_ref[2:3, cols], 1.0, 0.0)
            inc[pl.ds(base, step_rows), at : at + LANES] = (second - first).astype(BF16)
            inc[pl.ds(base, step_rows), elems + at : elems + at + LANES] = (third - first).astype(BF16)
        return 0

    lax.fori_loop(0, slots // step_rows, fill, 0)

    fetch["order"].wait()
    row = order_ref[...]
    row = jnp.where(harm == 0, row, jnp.concatenate([row[:, block:], row[:, :block]], axis=1))
    lanes = lax.broadcasted_iota(jnp.int32, (ncoef, ncoef), 1)
    subs = lax.broadcasted_iota(jnp.int32, (ncoef, ncoef), 0)
    synth3 = in_three(wave(row, subs, ncoef))
    column = jnp.sum(jnp.where(lanes == subs, row.astype(F32), 0.0), axis=1, keepdims=True)
    column = column.astype(jnp.int32)
    weight = jnp.where((column == 0) | (column == ncoef - 1), 1.0, 2.0) / ncoef
    proj3 = in_three(wave(column, lanes, ncoef) * weight)
    freq = (OMEGA * ((column[0:block] + 1) // 2).astype(F32)) ** 2

    for at in range(0, 2 * elems, LANES):
        edge_own[:, at : at + LANES] = dot(own_hl[...], inc[0:nodes, at : at + LANES])

    coef_copy.wait_recv()
    high, lower = halves(coef_in[...])
    other_hl[0:rows, 0:nodes] = high
    other_hl[rows : 2 * rows, 0:nodes] = lower
    border_wait_recv(*ghost_args, 0)
    border_wait_recv(*ghost_args, 1)
    high, lower = halves(unpack_border(ghost_in[0, 0], ghost_in[1, 0]))
    ghost_hl[0:rows, :] = high
    ghost_hl[rows : 2 * rows, :] = lower
    high, lower = halves(unpack_border(ghost_in[0, 1], ghost_in[1, 1]))
    other_hl[0:rows, nodes:slots] = high
    other_hl[rows : 2 * rows, nodes:slots] = lower

    for at in range(0, 2 * elems, LANES):
        cols = slice(at, at + LANES)
        mine_edges = edge_own[:, cols] + dot(ghost_hl[...], inc[nodes:slots, cols])
        other_edges = dot(other_hl[...], inc[:, cols])
        for half, edges in enumerate((mine_edges, other_edges)):
            high, lower = halves(edges[0:rows] + edges[rows : 2 * rows])
            for c in range(3):
                part = slice(c * block, (c + 1) * block)
                for third, piece in enumerate((high, lower, high)):
                    top = third * ncoef + half * block
                    edge_hl[c, top : top + block, cols] = piece[part]
    for c in range(3):
        for at in range(0, 2 * elems, LANES):
            cols = slice(at, at + LANES)
            disp[c, :, cols] = dot(synth3, edge_hl[c, :, cols])

    fetch["edge"].wait()
    fetch["stiff"].wait()
    def sample_rows(k, _):
        base = pl.multiple_of(k * 16, 16)
        times = pl.ds(base, 16)
        for at in range(0, elems, LANES):
            cols = pl.ds(pl.multiple_of(harm * elems + at, LANES), LANES)
            stiff = stiff_ref[0:1, cols]
            refs_b = [edge_ref[c, 0:1, cols] for c in range(3)]
            refs_c = [edge_ref[c, 1:2, cols] for c in range(3)]
            refs_d = [x - y for x, y in zip(refs_c, refs_b)]

            def pull(stretch, refs):
                rest = refs[0] * refs[0] + refs[1] * refs[1] + refs[2] * refs[2]
                square = stretch[0] * stretch[0] + stretch[1] * stretch[1] + stretch[2] * stretch[2]
                return stiff * (0.5 * (square - rest) + PRESTRESS)

            str_b = [refs_b[c] + disp[c, times, at : at + LANES] for c in range(3)]
            str_c = [refs_c[c] + disp[c, times, elems + at : elems + at + LANES] for c in range(3)]
            str_d = [x - y for x, y in zip(str_c, str_b)]
            ten_b = pull(str_b, refs_b)
            ten_c = pull(str_c, refs_c)
            ten_d = pull(str_d, refs_d)
            for c in range(3):
                mid = ten_d * str_d[c]
                for which, value in enumerate((ten_b * str_b[c] - mid, ten_c * str_c[c] + mid)):
                    high, lower = halves(value)
                    to = slice(which * elems + at, which * elems + at + LANES)
                    force_hl[c, times, to] = high
                    force_hl[c, pl.ds(base + ncoef, 16), to] = lower
                    force_hl[c, pl.ds(base + 2 * ncoef, 16), to] = high
        return 0

    lax.fori_loop(0, ncoef // 16, sample_rows, 0)

    for c in range(3):
        for at in range(0, 2 * elems, LANES):
            cols = slice(at, at + LANES)
            value = dot(proj3, force_hl[c, :, cols])
            high, lower = halves(value)
            for half in (0, 1):
                part = slice(half * block, (half + 1) * block)
                coef_hl[half, c * block : (c + 1) * block, cols] = high[part]
                coef_hl[half, rows + c * block : rows + (c + 1) * block, cols] = lower[part]

    def spread(half, start, stop):
        summed = dot_t(coef_hl[half], inc[start:stop, :])
        return summed[0:rows] + summed[rows : 2 * rows]

    back_args = [
        (back_out.at[rel], back_in, back_send_sem, back_recv_sem, rel) for rel in (0, 1)
    ]
    back_out[1, 1], back_out[1, 0] = pack_border(spread(1, nodes, slots))
    border_start(*back_args[1])
    back_out[0, 1], back_out[0, 0] = pack_border(spread(0, nodes, slots))
    border_start(*back_args[0])
    for at in range(0, nodes, LANES):
        part_out[:, at : at + LANES] = spread(1, at, at + LANES)
    part_copy = pltpu.make_async_remote_copy(
        src_ref=part_out, dst_ref=part_in, send_sem=part_sem.at[0], recv_sem=part_sem.at[1],
        device_id={"harm": other}, device_id_type=MESH,
    )
    part_copy.start()
    fetch["load"].wait()
    fetch["mass"].wait()
    for at in range(0, nodes, LANES):
        cols = slice(at, at + LANES)
        forces = spread(0, at, at + LANES)
        for c in range(3):
            part = slice(c * block, (c + 1) * block)
            inertia = freq * mass_ref[0:1, cols] * coef_ref[part, cols]
            main_own[part, cols] = forces[part] - inertia - load_ref[part, cols]
    fetch["basis"].wait()

    border_wait_recv(*back_args[0])
    border_wait_recv(*back_args[1])
    back = unpack_border(back_in[1, 0] + back_in[1, 1], back_in[0, 0] + back_in[0, 1])
    high, lower = halves(back)
    ghost_hl[0:rows, :] = high
    ghost_hl[rows : 2 * rows, :] = lower
    part_copy.wait_recv()
    for at in range(0, nodes, LANES):
        cols = slice(at, at + LANES)
        added = dot_t(ghost_hl[...], pick[at : at + LANES, :])
        forces = main_own[:, cols] + part_in[:, cols] + (added[0:rows] + added[rows : 2 * rows])
        for c in range(3):
            part = slice(c * block, (c + 1) * block)
            value = forces[part]
            resid_ref[part, cols] = value
            low[c, :, cols] = value.astype(BF16)

    total = None
    for c in range(3):
        term = dot_t(basis_ref[c], low[c])
        total = term if total is None else total + term
    for piece in range(n_mesh):
        prod_out[piece] = jnp.concatenate(
            [total[piece * share + q * sub : piece * share + (q + 1) * sub] for q in range(fold)], axis=1
        )

    prod_copies = []
    for step in range(1, n_mesh):
        peer = lax.rem(me + step, n_mesh)
        copy = pltpu.make_async_remote_copy(
            src_ref=prod_out.at[peer], dst_ref=prod_in.at[step - 1],
            send_sem=prod_send_sem.at[step - 1], recv_sem=prod_recv_sem.at[step - 1],
            device_id={"mesh": peer}, device_id_type=MESH,
        )
        copy.start()
        prod_copies.append(copy)

    coef_copy.wait_send()
    part_copy.wait_send()
    for rel in (0, 1):
        border_wait_send(*ghost_args, rel)
        border_wait_send(*back_args[rel])
    for copy in prod_copies:
        copy.wait_recv()
    result = prod_out[me]
    for step in range(1, n_mesh):
        result = result + prod_in[step - 1]
    for q in range(fold):
        reduced_ref[q * sub : (q + 1) * sub, :] = result[:, q * block : (q + 1) * block]
    for copy in prod_copies:
        copy.wait_send()


def per_device(coeffs, load, mass, stiffness, edge_ref, conn, ghost_send, order, basis):
    n_mesh = lax.axis_size("mesh")
    block, _, nodes = coeffs.shape
    rows = 3 * block
    ncoef = 2 * block
    elems = conn.shape[1] // 2
    ghosts = ghost_send.shape[1]
    slots = nodes + 2 * ghosts
    basis_count = basis.shape[0]
    share = basis_count // n_mesh
    fold = min(128 // block, share)
    vmem = pl.BlockSpec(memory_space=pltpu.VMEM)
    hbm = pl.BlockSpec(memory_space=pltpu.HBM)
    dma = pltpu.SemaphoreType.DMA

    def body(*refs):
        kernel(n_mesh, *refs)

    resid, reduced = pl.pallas_call(
        body,
        out_shape=(
            jax.ShapeDtypeStruct((rows, nodes), F32),
            jax.ShapeDtypeStruct((share, block), F32),
        ),
        in_specs=[hbm] * 9,
        out_specs=(vmem, vmem),
        scratch_shapes=[
            pltpu.VMEM((rows, nodes), F32),
            pltpu.VMEM((rows, nodes), F32),
            pltpu.VMEM((1, nodes), F32),
            pltpu.VMEM((1, 2 * elems), F32),
            pltpu.VMEM((3, 2, 2 * elems), F32),
            pltpu.VMEM((3, 2 * elems), jnp.int32),
            pltpu.VMEM((2, ghosts), jnp.int32),
            pltpu.VMEM((1, ncoef), jnp.int32),
            pltpu.VMEM((3, basis_count, nodes), BF16),
            pltpu.VMEM((rows, nodes), F32),
            pltpu.VMEM((2 * rows, nodes), BF16),
            pltpu.VMEM((2 * rows, slots), BF16),
            pltpu.VMEM((nodes, 2 * ghosts), BF16),
            pltpu.VMEM((slots, 2 * elems), BF16),
            pltpu.VMEM((2, rows // 2, 2 * ghosts), F32),
            pltpu.VMEM((2, 2, rows // 2, 2 * ghosts), F32),
            pltpu.VMEM((2 * rows, 2 * ghosts), BF16),
            pltpu.VMEM((2 * rows, 2 * elems), F32),
            pltpu.VMEM((3, 3 * ncoef, 2 * elems), BF16),
            pltpu.VMEM((3, ncoef, 2 * elems), F32),
            pltpu.VMEM((3, 3 * ncoef, 2 * elems), BF16),
            pltpu.VMEM((2, 2 * rows, 2 * elems), BF16),
            pltpu.VMEM((2, 2, rows // 2, 2 * ghosts), F32),
            pltpu.VMEM((2, 2, rows // 2, 2 * ghosts), F32),
            pltpu.VMEM((rows, nodes), F32),
            pltpu.VMEM((rows, nodes), F32),
            pltpu.VMEM((rows, nodes), F32),
            pltpu.VMEM((3, block, nodes), BF16),
            pltpu.VMEM((n_mesh, share // fold, fold * block), F32),
            pltpu.VMEM((n_mesh - 1, share // fold, fold * block), F32),
            dma((9,)),
            dma((2,)),
            dma((2, 2)),
            dma((2, 2)),
            dma((2,)),
            dma((2, 2)),
            dma((2, 2)),
            dma((n_mesh - 1,)),
            dma((n_mesh - 1,)),
        ],
        compiler_params=pltpu.CompilerParams(
            collective_id=0, has_side_effects=True, vmem_limit_bytes=60 * 1024 * 1024
        ),
    )(
        coeffs.transpose(1, 0, 2).reshape(rows, nodes),
        load.transpose(1, 0, 2).reshape(rows, nodes),
        mass.reshape(1, -1),
        stiffness.reshape(1, -1),
        edge_ref.transpose(1, 0, 2),
        conn,
        ghost_send,
        order.reshape(1, -1),
        basis.transpose(1, 0, 2),
    )
    return resid.reshape(3, block, nodes).transpose(1, 0, 2), reduced


def solution(mesh):
    in_specs = (
        P("harm", None, ("case", "mesh")),
        P("harm", None, ("case", "mesh")),
        P("mesh"),
        P("mesh"),
        P(None, None, "mesh"),
        P(None, "mesh"),
        P(None, "mesh"),
        P(),
        P(None, None, "mesh"),
    )
    out_specs = (P("harm", None, ("case", "mesh")), P("mesh", ("case", "harm")))
    return jax.shard_map(
        per_device, mesh=mesh, in_specs=in_specs, out_specs=out_specs, check_vma=False
    )
```
